32 devices in a mesh: grp: 2 (over x), gx: 16 (over z, y, core).
Axes of the slice: x: 2, y: 2, z: 4, core: 2. Of those that a mesh axis runs over, the one named last changes fastest.
Arguments:
- saved_field: bfloat16 [128, 128, 512], P(('grp', 'gx')), parts along dimension 0, may hold values from -6 to 6
- right_side: float32 [128, 128, 512], P(('grp', 'gx')), parts along dimension 0, may hold values from -6 to 6
- face_x: float32 [128, 128, 512], P(('grp', 'gx')), parts along dimension 0, may hold values from 0.1 to 10
- face_y: float32 [128, 128, 512], P(('grp', 'gx')), parts along dimension 0, may hold values from 0.1 to 10
- face_z: float32 [128, 128, 512], P(('grp', 'gx')), parts along dimension 0, may hold values from 0.1 to 10
- cotangent: float32 [128, 128, 512], P(('grp', 'gx')), parts along dimension 0, may hold values from -6 to 6
Outputs:
- adjoint_field: float32 [128, 128, 512], P(('grp', 'gx')), parts along dimension 0
- grad_x: float32 [128, 128, 512], P(('grp', 'gx')), parts along dimension 0
- grad_y: float32 [128, 128, 512], P(('grp', 'gx')), parts along dimension 0
- grad_z: float32 [128, 128, 512], P(('grp', 'gx')), parts along dimension 0
The draws below stay inside these ranges and needn't reach their ends.
There are 2 independent parts, one for each index of `grp`. The reference program is written for one: setup_inputs(seed, part) draws one part's arguments, and reference() takes and returns one part's arrays. A program takes and returns all parts, laid end to end along the dimension named above; each array names one. Nothing has to cross between parts.
All inputs are finite; a program needn't handle non-finite values.
Results may differ from the reference program's by a relative error of at most 0.0003.
Values sent between devices are 32-bit elements; how exact they have to be, the bound alone decides.
A program may use at most 64 MiB of HBM per device.

```python
import math
import jax
import jax.numpy as jnp

NY = 128
NZ = 512
STEPS = 4
NX = 64


def block_scale(stream_key, extent, pieces, smallest, largest):
    loudness = 1.0
    for dim, parts in pieces:
        draws = jax.random.uniform(jax.random.fold_in(jax.random.fold_in(stream_key, 6), dim), (parts,), jnp.float32, smallest / len(pieces), largest / len(pieces))
        loudness = loudness * jnp.repeat(jnp.exp(draws), extent[dim] // parts).reshape((-1,) + (1,) * (len(extent) - 1 - dim))
    return loudness


def centred(key, shape, width, limit, split=(), dtype=jnp.bfloat16):
    result = jax.random.normal(key, shape, jnp.float32) * width
    if len(split) > 0:
        result = block_scale(key, shape, split, -0.22, 0.18) * result
    return jnp.clip(result, min=-limit, max=limit).astype(dtype)


def setup_inputs(seed: int = 0, part: int = 0) -> dict:
    keys = jax.random.split(jax.random.key(seed), 7)
    part_splits = jax.random.split(jax.random.fold_in(keys[6], part), 7)
    saved_field = centred(part_splits[0], (NX, NY, NZ), 1.0, 6.0, ((0, 16),))
    right_side = centred(part_splits[1], (NX, NY, NZ), 1.0, 6.0, ((0, 16),), jnp.float32)
    face_x = jnp.clip(jnp.exp(math.log(10.0) - 4.6051702 * jax.random.uniform(part_splits[2], (NX, NY, NZ), jnp.float32) ** block_scale(part_splits[2], (NX, NY, NZ), ((0, 16),), -0.2, 0.2)), 0.1, 10.0)
    face_y = jnp.clip(jnp.exp(math.log(10.0) - 4.6051702 * jax.random.uniform(part_splits[3], (NX, NY, NZ), jnp.float32) ** block_scale(part_splits[3], (NX, NY, NZ), ((0, 16),), -0.2, 0.2)), 0.1, 10.0)
    face_z = jnp.clip(jnp.exp(math.log(10.0) - 4.6051702 * jax.random.uniform(part_splits[4], (NX, NY, NZ), jnp.float32) ** block_scale(part_splits[4], (NX, NY, NZ), ((0, 16),), -0.2, 0.2)), 0.1, 10.0)
    cotangent = centred(part_splits[5], (NX, NY, NZ), 1.0, 6.0, ((0, 16),), jnp.float32)
    return dict(saved_field=saved_field, right_side=right_side, face_x=face_x, face_y=face_y, face_z=face_z, cotangent=cotangent)


spectrum_low = 0.25
spectrum_high = 2.05

def chebyshev(count):
    centre = (spectrum_high + spectrum_low) / 2.0
    half = (spectrum_high - spectrum_low) / 2.0
    ratio = centre / half
    rho_prev = 1.0 / ratio
    coefs = [(0.0, 1.0 / centre)]
    for index in range(1, count):
        rho_next = 1.0 / (2.0 * ratio - rho_prev)
        coefs.append((rho_next * rho_prev, 2.0 * rho_next / half))
        rho_prev = rho_next
    return coefs

def lower_along(values, axis):
    widths = [(0, 0), (0, 0), (0, 0)]
    widths[axis] = (1, 0)
    return jax.lax.slice_in_dim(jnp.pad(values, widths), 0, values.shape[axis], axis=axis)

def upper_along(values, axis):
    widths = [(0, 0), (0, 0), (0, 0)]
    widths[axis] = (0, 1)
    return jax.lax.slice_in_dim(jnp.pad(values, widths), 1, values.shape[axis] + 1, axis=axis)

def operate(field, face_x, face_y, face_z):
    flow = face_x * (field - lower_along(field, 0)) + upper_along(face_x, 0) * (field - upper_along(field, 0))
    flow = flow + face_y * (field - lower_along(field, 1)) + upper_along(face_y, 1) * (field - upper_along(field, 1))
    flow = flow + face_z * (field - lower_along(field, 2)) + upper_along(face_z, 2) * (field - upper_along(field, 2))
    return flow

def forward(start, right_side, face_x, face_y, face_z):
    coefs = chebyshev(STEPS)
    diagonal = face_x + upper_along(face_x, 0) + face_y + upper_along(face_y, 1) + face_z + upper_along(face_z, 2)
    field = start
    previous = jnp.zeros_like(start)
    for step in range(STEPS):
        scaled = (right_side - operate(field, face_x, face_y, face_z)) / diagonal
        if step == 0:
            change = coefs[0][1] * scaled
        else:
            change = coefs[step][0] * previous + coefs[step][1] * scaled
        field = field + change
        previous = change
    return field

def reference(saved_field, right_side, face_x, face_y, face_z, cotangent):
    start = saved_field.astype(jnp.float32)

    def closed(first, fx, fy, fz):
        return forward(first, right_side, fx, fy, fz)
    output, pullback = jax.vjp(closed, start, face_x, face_y, face_z)
    adjoint_field, grad_x, grad_y, grad_z = pullback(cotangent)
    return (adjoint_field, grad_x, grad_y, grad_z)
```

```python
import jax
import jax.numpy as jnp
from jax import lax
from jax.experimental import pallas as pl
from jax.experimental.pallas import tpu as pltpu
from jax.sharding import PartitionSpec as P

STEPS = 4
ROWS = 16
PAD = 8

spectrum_low = 0.25
spectrum_high = 2.05


def chebyshev(count):
    centre = (spectrum_high + spectrum_low) / 2.0
    half = (spectrum_high - spectrum_low) / 2.0
    ratio = centre / half
    rho_prev = 1.0 / ratio
    coefs = [(0.0, 1.0 / centre)]
    for index in range(1, count):
        rho_next = 1.0 / (2.0 * ratio - rho_prev)
        coefs.append((rho_next * rho_prev, 2.0 * rho_next / half))
        rho_prev = rho_next
    return coefs


def make_kernel(n, layers, ny, nz):
    coefs = chebyshev(STEPS)
    top = layers
    high = layers + 1
    last = STEPS - 1
    f32 = jnp.float32

    def kernel(saved_h, rhs_h, fx_h, fy_h, fz_h, cot_h, adj_o, gx_o, gy_o, gz_o,
               u, p, fx, fy, fz, rd, rhs, d, cb, adj, z, gx, gy, gz, db, raw,
               in_sem, out_sem, send_sem, recv_sem, edge_send, edge_recv):
        me = lax.axis_index("gx")
        core = me % 2
        near, far = me + 1 - 2 * core, me - 1 + 2 * core
        near_layer, far_layer = top - (top - 1) * core, 1 + (top - 1) * core
        near_halo, far_halo = high * (1 - core), high * core
        has_far = jnp.logical_and(far >= 0, far < n)
        has_below, has_above = me > 0, me < n - 1
        data = pl.ds(PAD, ny)

        loads = [
            pltpu.make_async_copy(saved_h, raw, in_sem.at[0]),
            pltpu.make_async_copy(fx_h, fx.at[pl.ds(0, layers)], in_sem.at[1]),
            pltpu.make_async_copy(cot_h, adj, in_sem.at[2]),
            pltpu.make_async_copy(fy_h, fy.at[:, data], in_sem.at[3]),
            pltpu.make_async_copy(fz_h, fz, in_sem.at[4]),
            pltpu.make_async_copy(rhs_h, rhs, in_sem.at[5]),
        ]
        for load in loads:
            load.start()

        barrier = pltpu.get_barrier_semaphore()
        pl.semaphore_signal(barrier, inc=1, device_id={"gx": near},
                            device_id_type=pl.DeviceIdType.MESH)

        @pl.when(has_far)
        def _():
            pl.semaphore_signal(barrier, inc=1, device_id={"gx": far},
                                device_id_type=pl.DeviceIdType.MESH)

        def halo(buf, which, k, side):
            layer, there, device = (
                (near_layer, high - near_halo, near) if side == 0
                else (far_layer, high - far_halo, far)
            )
            return pltpu.make_async_remote_copy(
                src_ref=buf.at[k, layer, data],
                dst_ref=buf.at[k, there, data],
                send_sem=send_sem.at[which, k, side],
                recv_sem=recv_sem.at[which, k, side],
                device_id={"gx": device},
                device_id_type=pl.DeviceIdType.MESH,
            )

        def on_side(side, action):
            if side == 0:
                action()
            else:
                pl.when(has_far)(action)

        def send(buf, which, k, side):
            on_side(side, lambda: halo(buf, which, k, side).start())

        def receive(buf, which, k, side):
            on_side(side, lambda: halo(buf, which, k, side).wait_recv())

        face_copy = pltpu.make_async_remote_copy(
            src_ref=fx.at[0], dst_ref=fx.at[layers],
            send_sem=edge_send.at[0], recv_sem=edge_recv.at[0],
            device_id={"gx": me - 1}, device_id_type=pl.DeviceIdType.MESH)
        diag_copy = pltpu.make_async_remote_copy(
            src_ref=db.at[top, data], dst_ref=db.at[0, data],
            send_sem=edge_send.at[1], recv_sem=edge_recv.at[1],
            device_id={"gx": me + 1}, device_id_type=pl.DeviceIdType.MESH)

        strip = jnp.zeros((PAD, nz), f32)

        def clear_pads(l, carry):
            for k in range(STEPS):
                for buf in (u, p):
                    buf[k, l + 1, pl.ds(0, PAD), :] = strip
                    buf[k, l + 1, pl.ds(PAD + ny, PAD), :] = strip
            fy[l, pl.ds(PAD + ny, PAD), :] = strip
            db[l + 1, pl.ds(0, PAD), :] = strip
            return carry

        lax.fori_loop(0, layers, clear_pads, 0)

        @pl.when(jnp.logical_not(has_far))
        def _():
            def clear(r, carry):
                for k in range(STEPS):
                    for buf in (u, p):
                        buf[k, far_halo, pl.ds(PAD + r * PAD, PAD), :] = strip
                return carry

            lax.fori_loop(0, ny // PAD, clear, 0)

        @pl.when(jnp.logical_not(has_above))
        def _():
            def clear(r, carry):
                fx[layers, pl.ds(r * PAD, PAD), :] = strip
                return carry

            lax.fori_loop(0, ny // PAD, clear, 0)

        @pl.when(jnp.logical_not(has_below))
        def _():
            def clear(r, carry):
                db[0, pl.ds(PAD + r * PAD, PAD), :] = strip
                return carry

            lax.fori_loop(0, ny // PAD, clear, 0)

        lane = lax.broadcasted_iota(jnp.int32, (ROWS, nz), 1)
        first_lane, last_lane = lane == 0, lane == nz - 1

        def lower_z(x):
            return jnp.where(first_lane, 0.0, pltpu.roll(x, 1, 1))

        def upper_z(x):
            return jnp.where(last_lane, 0.0, pltpu.roll(x, nz - 1, 1))

        def lower_y(load, r):
            tall = load(pl.ds(pl.multiple_of(r, PAD), ROWS + PAD))
            return pltpu.roll(tall, 1, 0)[PAD:]

        def upper_y(load, r):
            tall = load(pl.ds(pl.multiple_of(PAD + r, PAD), ROWS + PAD))
            return pltpu.roll(tall, ROWS + PAD - 1, 0)[:ROWS]

        def over_rows(body):
            def step(i, carry):
                body(pl.multiple_of(i * ROWS, ROWS))
                return carry

            lax.fori_loop(0, ny // ROWS, step, 0)

        def stencil(buf, k, l, r):
            here = buf[k, l, pl.ds(PAD + r, ROWS), :]
            flow = fx[l - 1, pl.ds(r, ROWS), :] * (here - buf[k, l - 1, pl.ds(PAD + r, ROWS), :])
            flow += fx[l, pl.ds(r, ROWS), :] * (here - buf[k, l + 1, pl.ds(PAD + r, ROWS), :])
            flow += fy[l - 1, pl.ds(PAD + r, ROWS), :] * (
                here - lower_y(lambda i: buf[k, l, i, :], r))
            flow += upper_y(lambda i: fy[l - 1, i, :], r) * (
                here - upper_y(lambda i: buf[k, l, i, :], r))
            along = fz[l - 1, pl.ds(r, ROWS), :] * (here - lower_z(here))
            return here, flow + (along - upper_z(along))

        def widen(l):
            def body(r):
                u[0, l, pl.ds(PAD + r, ROWS), :] = raw[l - 1, pl.ds(r, ROWS), :].astype(f32)

            over_rows(body)

        def prepare(l):
            def body(r):
                rows = pl.ds(r, ROWS)
                across = fz[l - 1, rows, :]
                diagonal = (
                    fx[l - 1, rows, :] + fx[l, rows, :]
                    + fy[l - 1, pl.ds(PAD + r, ROWS), :]
                    + upper_y(lambda i: fy[l - 1, i, :], r)
                    + across + upper_z(across)
                )
                inverse = 1.0 / diagonal
                rd[l - 1, rows, :] = inverse
                seed = adj[l - 1, rows, :]
                cb[l - 1, rows, :] = seed
                p[last, l, pl.ds(PAD + r, ROWS), :] = (-coefs[last][1]) * seed * inverse

            over_rows(body)

        def forward(k, l):
            def body(r):
                rows = pl.ds(r, ROWS)
                here, flow = stencil(u, k, l, r)
                scaled = (rhs[l - 1, rows, :] - flow) * rd[l - 1, rows, :]
                z[k, l - 1, rows, :] = scaled
                if k < last:
                    change = coefs[k][1] * scaled
                    if k > 0:
                        change += coefs[k][0] * d[l - 1, rows, :]
                    d[l - 1, rows, :] = change
                    u[k + 1, l, pl.ds(PAD + r, ROWS), :] = here + change

            over_rows(body)

        def backward(k, l):
            def body(r):
                rows = pl.ds(r, ROWS)
                here, flow = stencil(p, k, l, r)
                total = adj[l - 1, rows, :] + flow
                adj[l - 1, rows, :] = total
                if k > 0:
                    change = total + coefs[k][0] * cb[l - 1, rows, :]
                    cb[l - 1, rows, :] = change
                    p[k - 1, l, pl.ds(PAD + r, ROWS), :] = (
                        (-coefs[k - 1][1]) * change * rd[l - 1, rows, :])

            over_rows(body)

        def grads(l, r, steps):
            sums = [None, None, None]
            for k in steps:
                mine = pl.ds(PAD + r, ROWS)
                a, b = u[k, l, mine, :], p[k, l, mine, :]
                terms = (
                    (a - u[k, l - 1, mine, :]) * (b - p[k, l - 1, mine, :]),
                    (a - lower_y(lambda i: u[k, l, i, :], r))
                    * (b - lower_y(lambda i: p[k, l, i, :], r)),
                    (a - lower_z(a)) * (b - lower_z(b)),
                )
                sums = [t if s is None else s + t for s, t in zip(sums, terms)]
            return sums

        def middle_grads(l):
            def body(r):
                rows = pl.ds(r, ROWS)
                for out, value in zip((gx, gy, gz), grads(l, r, (1, 2))):
                    out[l - 1, rows, :] = value

            over_rows(body)

        def diag_bar(l):
            def body(r):
                mine = pl.ds(PAD + r, ROWS)
                total = p[0, l, mine, :] * z[0, l - 1, pl.ds(r, ROWS), :]
                for k in range(1, STEPS):
                    total += p[k, l, mine, :] * z[k, l - 1, pl.ds(r, ROWS), :]
                db[l, mine, :] = total

            over_rows(body)

        def end_grads(l):
            def body(r):
                rows, mine = pl.ds(r, ROWS), pl.ds(PAD + r, ROWS)
                x, y, across = grads(l, r, (0, last))
                extra = db[l, mine, :]
                gx[l - 1, rows, :] += x + (extra + db[l - 1, mine, :])
                gy[l - 1, rows, :] += y + (extra + lower_y(lambda i: db[l, i, :], r))
                gz[l - 1, rows, :] += across + (extra + lower_z(extra))

            over_rows(body)

        def each_layer(first, end, action):
            def step(l, carry):
                action(l)
                return carry

            lax.fori_loop(first, end, step, 0)

        outs = ((adj, adj_o), (gx, gx_o), (gy, gy_o), (gz, gz_o))

        def stores(l, which):
            return [
                pltpu.make_async_copy(
                    outs[i][0].at[l - 1], outs[i][1].at[l - 1], out_sem.at[i, l - 1])
                for i in which
            ]

        loads[0].wait()
        each_layer(1, top + 1, widen)
        @pl.when(has_far)
        def _():
            pl.semaphore_wait(barrier, 2)

        @pl.when(jnp.logical_not(has_far))
        def _():
            pl.semaphore_wait(barrier, 1)

        loads[1].wait()
        pl.when(has_below)(face_copy.start)
        send(u, 0, 0, 0)
        send(u, 0, 0, 1)
        for load in loads[2:5]:
            load.wait()
        each_layer(1, top, prepare)
        pl.when(has_above)(face_copy.wait_recv)
        prepare(top)
        send(p, 1, last, 0)
        send(p, 1, last, 1)
        loads[5].wait()

        for k in range(last):
            back = last - k
            each_layer(2, top, lambda l: forward(k, l))
            for side, layer in ((0, near_layer), (1, far_layer)):
                receive(u, 0, k, side)
                forward(k, layer)
                send(u, 0, k + 1, side)
            each_layer(2, top, lambda l: backward(back, l))
            for side, layer in ((0, near_layer), (1, far_layer)):
                receive(p, 1, back, side)
                backward(back, layer)
                send(p, 1, back - 1, side)

        each_layer(2, top, lambda l: forward(last, l))
        each_layer(2, top, lambda l: backward(0, l))
        each_layer(1, top + 1, middle_grads)
        for side, layer in ((0, near_layer), (1, far_layer)):
            receive(u, 0, last, side)
            forward(last, layer)
        diag_bar(top)
        pl.when(has_above)(diag_copy.start)
        each_layer(1, top, diag_bar)
        each_layer(2, top + 1, end_grads)
        for l in range(2, top + 1):
            for store in stores(l, (1, 2, 3)):
                store.start()
        for side, layer in ((0, near_layer), (1, far_layer)):
            receive(p, 1, 0, side)
            backward(0, layer)
        for l in range(1, top + 1):
            stores(l, (0,))[0].start()
        pl.when(has_below)(diag_copy.wait_recv)
        end_grads(1)
        for store in stores(1, (1, 2, 3)):
            store.start()

        for which, buf in ((0, u), (1, p)):
            for k in range(STEPS):
                for side in range(2):
                    on_side(side, lambda: halo(buf, which, k, side).wait_send())
        pl.when(has_below)(face_copy.wait_send)
        pl.when(has_above)(diag_copy.wait_send)
        for l in range(1, top + 1):
            for store in stores(l, range(4)):
                store.wait()

    return kernel


def per_device(saved_field, right_side, face_x, face_y, face_z, cotangent):
    layers, ny, nz = face_x.shape
    n = lax.axis_size("gx")
    block = (layers, ny, nz)
    tall = ny + 2 * PAD

    def vmem(shape, dtype=jnp.float32):
        return pltpu.VMEM(shape, dtype)

    out = jax.ShapeDtypeStruct(block, jnp.float32)
    return pl.pallas_call(
        make_kernel(n, layers, ny, nz),
        out_shape=(out,) * 4,
        in_specs=[pl.BlockSpec(memory_space=pl.ANY)] * 6,
        out_specs=[pl.BlockSpec(memory_space=pl.ANY)] * 4,
        scratch_shapes=[
            vmem((STEPS, layers + 2, tall, nz)),
            vmem((STEPS, layers + 2, tall, nz)),
            vmem((layers + 1, ny, nz)),
            vmem((layers, tall, nz)),
            vmem(block),
            vmem(block),
            vmem(block),
            vmem(block),
            vmem(block),
            vmem(block),
            vmem((STEPS,) + block),
            vmem(block), vmem(block), vmem(block),
            vmem((layers + 1, tall, nz)),
            vmem(block, jnp.bfloat16),
            pltpu.SemaphoreType.DMA((6,)),
            pltpu.SemaphoreType.DMA((4, layers)),
            pltpu.SemaphoreType.DMA((2, STEPS, 2)),
            pltpu.SemaphoreType.DMA((2, STEPS, 2)),
            pltpu.SemaphoreType.DMA((2,)),
            pltpu.SemaphoreType.DMA((2,)),
        ],
        compiler_params=pltpu.CompilerParams(
            collective_id=0, has_side_effects=True, vmem_limit_bytes=48 * 1024 * 1024
        ),
        cost_estimate=pl.CostEstimate(
            flops=300 * layers * ny * nz, bytes_accessed=38 * layers * ny * nz, transcendentals=0
        ),
    )(saved_field, right_side, face_x, face_y, face_z, cotangent)


def solution(mesh):
    spec = P(("grp", "gx"), None, None)
    return jax.shard_map(
        per_device, mesh=mesh, in_specs=(spec,) * 6, out_specs=(spec,) * 4, check_vma=False
    )
```

```python
import jax
import jax.numpy as jnp
from jax import lax
from jax.experimental import pallas as pl
from jax.experimental.pallas import tpu as pltpu
from jax.sharding import PartitionSpec as P

STEPS = 4
ROWS = 64
PAD = 8

spectrum_low = 0.25
spectrum_high = 2.05


def chebyshev(count):
    centre = (spectrum_high + spectrum_low) / 2.0
    half = (spectrum_high - spectrum_low) / 2.0
    ratio = centre / half
    rho_prev = 1.0 / ratio
    coefs = [(0.0, 1.0 / centre)]
    for index in range(1, count):
        rho_next = 1.0 / (2.0 * ratio - rho_prev)
        coefs.append((rho_next * rho_prev, 2.0 * rho_next / half))
        rho_prev = rho_next
    return coefs


def make_kernel(n, layers, ny, nz):
    coefs = chebyshev(STEPS)
    top = layers
    high = layers + 1
    last = STEPS - 1
    f32 = jnp.float32

    def kernel(saved_h, rhs_h, fx_h, fy_h, fz_h, cot_h, adj_o, gx_o, gy_o, gz_o,
               u, p, fx, fy, fz, rd, rhs, d, cb, adj, z, gx, gy, gz, db, raw,
               in_sem, out_sem, send_sem, recv_sem, edge_send, edge_recv,
               diag_send, diag_recv):
        me = lax.axis_index("gx")
        core = me % 2
        near, far = me + 1 - 2 * core, me - 1 + 2 * core
        near_layer, far_layer = top - (top - 1) * core, 1 + (top - 1) * core
        near_halo, far_halo = high * (1 - core), high * core
        has_far = jnp.logical_and(far >= 0, far < n)
        has_below, has_above = me > 0, me < n - 1
        data = pl.ds(PAD, ny)

        loads = [
            pltpu.make_async_copy(saved_h, raw, in_sem.at[0]),
            pltpu.make_async_copy(fx_h, fx.at[pl.ds(0, layers)], in_sem.at[1]),
            pltpu.make_async_copy(cot_h, adj, in_sem.at[2]),
            pltpu.make_async_copy(fy_h, fy.at[:, data], in_sem.at[3]),
            pltpu.make_async_copy(fz_h, fz, in_sem.at[4]),
            pltpu.make_async_copy(rhs_h, rhs, in_sem.at[5]),
        ]
        for load in loads:
            load.start()

        barrier = pltpu.get_barrier_semaphore()
        pl.semaphore_signal(barrier, inc=1, device_id={"gx": near},
                            device_id_type=pl.DeviceIdType.MESH)

        @pl.when(has_far)
        def _():
            pl.semaphore_signal(barrier, inc=1, device_id={"gx": far},
                                device_id_type=pl.DeviceIdType.MESH)

        def halo(buf, which, k, side, c):
            layer, there, device = (
                (near_layer, high - near_halo, near) if side == 0
                else (far_layer, high - far_halo, far)
            )
            part = pl.ds(pl.multiple_of(PAD + c * ROWS, PAD), ROWS)
            return pltpu.make_async_remote_copy(
                src_ref=buf.at[k, layer, part],
                dst_ref=buf.at[k, there, part],
                send_sem=send_sem.at[which, k, side, c],
                recv_sem=recv_sem.at[which, k, side, c],
                device_id={"gx": device},
                device_id_type=pl.DeviceIdType.MESH,
            )

        def on_side(side, action):
            if side == 0:
                action()
            else:
                pl.when(has_far)(action)

        chunks = ny // ROWS

        def send(buf, which, k, side, c):
            on_side(side, lambda: halo(buf, which, k, side, c).start())

        def receive(buf, which, k, side, c):
            on_side(side, lambda: halo(buf, which, k, side, c).wait_recv())

        def each(first, end, action):
            def step(i, carry):
                action(i)
                return carry

            lax.fori_loop(first, end, step, 0)

        face_copy = pltpu.make_async_remote_copy(
            src_ref=fx.at[0], dst_ref=fx.at[layers],
            send_sem=edge_send.at[0], recv_sem=edge_recv.at[0],
            device_id={"gx": me - 1}, device_id_type=pl.DeviceIdType.MESH)
        def diag_copy(c):
            part = pl.ds(pl.multiple_of(PAD + c * ROWS, PAD), ROWS)
            return pltpu.make_async_remote_copy(
                src_ref=db.at[top, part], dst_ref=db.at[0, part],
                send_sem=diag_send.at[c], recv_sem=diag_recv.at[c],
                device_id={"gx": me + 1}, device_id_type=pl.DeviceIdType.MESH)

        strip = jnp.zeros((PAD, nz), f32)

        def clear_pads(l, carry):
            for k in range(STEPS):
                for buf in (u, p):
                    buf[k, l + 1, pl.ds(0, PAD), :] = strip
                    buf[k, l + 1, pl.ds(PAD + ny, PAD), :] = strip
            fy[l, pl.ds(PAD + ny, PAD), :] = strip
            db[l + 1, pl.ds(0, PAD), :] = strip
            return carry

        lax.fori_loop(0, layers, clear_pads, 0)

        @pl.when(jnp.logical_not(has_far))
        def _():
            def clear(r, carry):
                for k in range(STEPS):
                    for buf in (u, p):
                        buf[k, far_halo, pl.ds(PAD + r * PAD, PAD), :] = strip
                return carry

            lax.fori_loop(0, ny // PAD, clear, 0)

        @pl.when(jnp.logical_not(has_above))
        def _():
            def clear(r, carry):
                fx[layers, pl.ds(r * PAD, PAD), :] = strip
                return carry

            lax.fori_loop(0, ny // PAD, clear, 0)

        @pl.when(jnp.logical_not(has_below))
        def _():
            def clear(r, carry):
                db[0, pl.ds(PAD + r * PAD, PAD), :] = strip
                return carry

            lax.fori_loop(0, ny // PAD, clear, 0)

        lane = lax.broadcasted_iota(jnp.int32, (ROWS, nz), 1)
        first_lane, last_lane = lane == 0, lane == nz - 1

        def lower_z(x):
            return jnp.where(first_lane, 0.0, pltpu.roll(x, 1, 1))

        def upper_z(x):
            return jnp.where(last_lane, 0.0, pltpu.roll(x, nz - 1, 1))

        def lower_y(load, r):
            tall = load(pl.ds(pl.multiple_of(r, PAD), ROWS + PAD))
            return pltpu.roll(tall, 1, 0)[PAD:]

        def upper_y(load, r):
            tall = load(pl.ds(pl.multiple_of(PAD + r, PAD), ROWS + PAD))
            return pltpu.roll(tall, ROWS + PAD - 1, 0)[:ROWS]

        def over_rows(body, l):
            each(0, chunks, lambda c: body(l, pl.multiple_of(c * ROWS, ROWS), c))

        def stencil(buf, k, l, r):
            here = buf[k, l, pl.ds(PAD + r, ROWS), :]
            flow = fx[l - 1, pl.ds(r, ROWS), :] * (here - buf[k, l - 1, pl.ds(PAD + r, ROWS), :])
            flow += fx[l, pl.ds(r, ROWS), :] * (here - buf[k, l + 1, pl.ds(PAD + r, ROWS), :])
            flow += fy[l - 1, pl.ds(PAD + r, ROWS), :] * (
                here - lower_y(lambda i: buf[k, l, i, :], r))
            flow += upper_y(lambda i: fy[l - 1, i, :], r) * (
                here - upper_y(lambda i: buf[k, l, i, :], r))
            along = fz[l - 1, pl.ds(r, ROWS), :] * (here - lower_z(here))
            return here, flow + (along - upper_z(along))

        def widen(l, r):
            u[0, l, pl.ds(PAD + r, ROWS), :] = raw[l - 1, pl.ds(r, ROWS), :].astype(f32)

        def prepare(l, r):
            rows = pl.ds(r, ROWS)
            across = fz[l - 1, rows, :]
            diagonal = (
                fx[l - 1, rows, :] + fx[l, rows, :]
                + fy[l - 1, pl.ds(PAD + r, ROWS), :]
                + upper_y(lambda i: fy[l - 1, i, :], r)
                + across + upper_z(across)
            )
            inverse = 1.0 / diagonal
            rd[l - 1, rows, :] = inverse
            seed = adj[l - 1, rows, :]
            cb[l - 1, rows, :] = seed
            p[last, l, pl.ds(PAD + r, ROWS), :] = (-coefs[last][1]) * seed * inverse

        def forward(k, l, r):
            rows = pl.ds(r, ROWS)
            here, flow = stencil(u, k, l, r)
            scaled = (rhs[l - 1, rows, :] - flow) * rd[l - 1, rows, :]
            z[k, l - 1, rows, :] = scaled
            if k < last:
                change = coefs[k][1] * scaled
                if k > 0:
                    change += coefs[k][0] * d[l - 1, rows, :]
                d[l - 1, rows, :] = change
                u[k + 1, l, pl.ds(PAD + r, ROWS), :] = here + change

        def backward(k, l, r):
            rows = pl.ds(r, ROWS)
            here, flow = stencil(p, k, l, r)
            total = adj[l - 1, rows, :] + flow
            adj[l - 1, rows, :] = total
            if k > 0:
                change = total + coefs[k][0] * cb[l - 1, rows, :]
                cb[l - 1, rows, :] = change
                p[k - 1, l, pl.ds(PAD + r, ROWS), :] = (
                    (-coefs[k - 1][1]) * change * rd[l - 1, rows, :])

        def grads(l, r, steps):
            sums = [None, None, None]
            for k in steps:
                mine = pl.ds(PAD + r, ROWS)
                a, b = u[k, l, mine, :], p[k, l, mine, :]
                terms = (
                    (a - u[k, l - 1, mine, :]) * (b - p[k, l - 1, mine, :]),
                    (a - lower_y(lambda i: u[k, l, i, :], r))
                    * (b - lower_y(lambda i: p[k, l, i, :], r)),
                    (a - lower_z(a)) * (b - lower_z(b)),
                )
                sums = [t if s is None else s + t for s, t in zip(sums, terms)]
            return sums

        def middle_grads(l, r):
            rows = pl.ds(r, ROWS)
            for out, value in zip((gx, gy, gz), grads(l, r, (1, 2))):
                out[l - 1, rows, :] = value

        def diag_bar(l, r):
            mine = pl.ds(PAD + r, ROWS)
            total = p[0, l, mine, :] * z[0, l - 1, pl.ds(r, ROWS), :]
            for k in range(1, STEPS):
                total += p[k, l, mine, :] * z[k, l - 1, pl.ds(r, ROWS), :]
            db[l, mine, :] = total

        def end_grads(l, r):
            rows, mine = pl.ds(r, ROWS), pl.ds(PAD + r, ROWS)
            x, y, across = grads(l, r, (0, last))
            extra = db[l, mine, :]
            gx[l - 1, rows, :] += x + (extra + db[l - 1, mine, :])
            gy[l - 1, rows, :] += y + (extra + lower_y(lambda i: db[l, i, :], r))
            gz[l - 1, rows, :] += across + (extra + lower_z(extra))

        def rows_of(action, l):
            each(0, chunks, lambda c: action(l, pl.multiple_of(c * ROWS, ROWS)))

        def layers_of(first, end, action):
            each(first, end, lambda l: rows_of(action, l))

        def first_send(buf, which, k):
            for side in range(2):
                each(0, chunks, lambda c: send(buf, which, k, side, c))

        outs = ((adj, adj_o), (gx, gx_o), (gy, gy_o), (gz, gz_o))

        def stores(l, which):
            return [
                pltpu.make_async_copy(
                    outs[i][0].at[l - 1], outs[i][1].at[l - 1], out_sem.at[i, l - 1])
                for i in which
            ]

        loads[0].wait()
        layers_of(1, top + 1, widen)
        @pl.when(has_far)
        def _():
            pl.semaphore_wait(barrier, 2)

        @pl.when(jnp.logical_not(has_far))
        def _():
            pl.semaphore_wait(barrier, 1)

        loads[1].wait()
        pl.when(has_below)(face_copy.start)
        first_send(u, 0, 0)
        for load in loads[2:5]:
            load.wait()
        layers_of(1, top, prepare)
        pl.when(has_above)(face_copy.wait_recv)
        rows_of(prepare, top)
        first_send(p, 1, last)
        loads[5].wait()

        def halo_step(k, side, layer, buf, which, step, following):
            def chunk(c):
                receive(buf, which, k, side, c)
                step(k, layer, pl.multiple_of(c * ROWS, ROWS))
                if following is not None:
                    send(buf, which, following, side, c)

            each(0, chunks, chunk)

        for k in range(last):
            back = last - k
            layers_of(2, top, lambda l, r: forward(k, l, r))
            layers_of(2, top, lambda l, r: backward(back, l, r))
            for side, layer in ((0, near_layer), (1, far_layer)):
                halo_step(k, side, layer, u, 0, forward, k + 1)
                halo_step(back, side, layer, p, 1, backward, back - 1)

        def store(l, which):
            for copy in stores(l, which):
                copy.start()

        def finish(l):
            rows_of(end_grads, l)
            store(l, (1, 2, 3))

        def close(k, l, r):
            forward(k, l, r)
            diag_bar(l, r)

        def close_backward(l):
            store(l, (0,))

        layers_of(2, top, lambda l, r: close(last, l, r))
        layers_of(2, top, lambda l, r: backward(0, l, r))
        layers_of(1, top + 1, middle_grads)
        each(2, top, close_backward)
        halo_step(last, 0, near_layer, u, 0, close, None)

        @pl.when(jnp.logical_and(core == 0, has_above))
        def _():
            each(0, chunks, lambda c: diag_copy(c).start())

        halo_step(0, 0, near_layer, p, 1, backward, None)
        store(near_layer, (0,))
        each(3 - core, top + 1 - core, finish)

        def far_chunk(c):
            receive(u, 0, last, 1, c)
            close(last, far_layer, pl.multiple_of(c * ROWS, ROWS))

            @pl.when(jnp.logical_and(core == 1, has_above))
            def _():
                diag_copy(c).start()

        each(0, chunks, far_chunk)
        finish(2 + (top - 2) * core)
        halo_step(0, 1, far_layer, p, 1, backward, None)
        store(far_layer, (0,))

        def last_chunk(c):
            @pl.when(has_below)
            def _():
                diag_copy(c).wait_recv()

            end_grads(1, pl.multiple_of(c * ROWS, ROWS))

        each(0, chunks, last_chunk)
        store(1, (1, 2, 3))

        for which, buf in ((0, u), (1, p)):
            for k in range(STEPS):
                for side in range(2):
                    each(0, chunks, lambda c: on_side(
                        side, lambda: halo(buf, which, k, side, c).wait_send()))
        pl.when(has_below)(face_copy.wait_send)

        @pl.when(has_above)
        def _():
            each(0, chunks, lambda c: diag_copy(c).wait_send())

        def wait_stores(l):
            for copy in stores(l, range(4)):
                copy.wait()

        each(1, top + 1, wait_stores)

    return kernel


def per_device(saved_field, right_side, face_x, face_y, face_z, cotangent):
    layers, ny, nz = face_x.shape
    n = lax.axis_size("gx")
    block = (layers, ny, nz)
    tall = ny + 2 * PAD

    def vmem(shape, dtype=jnp.float32):
        return pltpu.VMEM(shape, dtype)

    out = jax.ShapeDtypeStruct(block, jnp.float32)
    return pl.pallas_call(
        make_kernel(n, layers, ny, nz),
        out_shape=(out,) * 4,
        in_specs=[pl.BlockSpec(memory_space=pl.ANY)] * 6,
        out_specs=[pl.BlockSpec(memory_space=pl.ANY)] * 4,
        scratch_shapes=[
            vmem((STEPS, layers + 2, tall, nz)),
            vmem((STEPS, layers + 2, tall, nz)),
            vmem((layers + 1, ny, nz)),
            vmem((layers, tall, nz)),
            vmem(block),
            vmem(block),
            vmem(block),
            vmem(block),
            vmem(block),
            vmem(block),
            vmem((STEPS,) + block),
            vmem(block), vmem(block), vmem(block),
            vmem((layers + 1, tall, nz)),
            vmem(block, jnp.bfloat16),
            pltpu.SemaphoreType.DMA((6,)),
            pltpu.SemaphoreType.DMA((4, layers)),
            pltpu.SemaphoreType.DMA((2, STEPS, 2, ny // ROWS)),
            pltpu.SemaphoreType.DMA((2, STEPS, 2, ny // ROWS)),
            pltpu.SemaphoreType.DMA((1,)),
            pltpu.SemaphoreType.DMA((1,)),
            pltpu.SemaphoreType.DMA((ny // ROWS,)),
            pltpu.SemaphoreType.DMA((ny // ROWS,)),
        ],
        compiler_params=pltpu.CompilerParams(
            collective_id=0, has_side_effects=True, vmem_limit_bytes=60 * 1024 * 1024
        ),
        cost_estimate=pl.CostEstimate(
            flops=300 * layers * ny * nz, bytes_accessed=38 * layers * ny * nz, transcendentals=0
        ),
    )(saved_field, right_side, face_x, face_y, face_z, cotangent)


def solution(mesh):
    spec = P(("grp", "gx"), None, None)
    return jax.shard_map(
        per_device, mesh=mesh, in_specs=(spec,) * 6, out_specs=(spec,) * 4, check_vma=False
    )
```

```python
import jax
import jax.numpy as jnp
from jax import lax
from jax.experimental import pallas as pl
from jax.experimental.pallas import tpu as pltpu
from jax.sharding import PartitionSpec as P

STEPS = 4
ROWS = 64
PAD = 8

spectrum_low = 0.25
spectrum_high = 2.05


def chebyshev(count):
    centre = (spectrum_high + spectrum_low) / 2.0
    half = (spectrum_high - spectrum_low) / 2.0
    ratio = centre / half
    rho_prev = 1.0 / ratio
    coefs = [(0.0, 1.0 / centre)]
    for index in range(1, count):
        rho_next = 1.0 / (2.0 * ratio - rho_prev)
        coefs.append((rho_next * rho_prev, 2.0 * rho_next / half))
        rho_prev = rho_next
    return coefs


def make_kernel(n, layers, ny, nz):
    coefs = chebyshev(STEPS)
    top = layers
    high = layers + 1
    last = STEPS - 1
    f32 = jnp.float32

    def kernel(saved_h, rhs_h, fx_h, fy_h, fz_h, cot_h, adj, gx, gy, gz,
               u, p, fx, fy, fz, rd, rhs, d, cb, z, db, raw,
               in_sem, send_sem, recv_sem, edge_send, edge_recv,
               diag_send, diag_recv):
        me = lax.axis_index("gx")
        core = me % 2
        near, far = me + 1 - 2 * core, me - 1 + 2 * core
        near_layer, far_layer = top - (top - 1) * core, 1 + (top - 1) * core
        near_halo, far_halo = high * (1 - core), high * core
        has_far = jnp.logical_and(far >= 0, far < n)
        has_below, has_above = me > 0, me < n - 1
        data = pl.ds(PAD, ny)

        loads = [
            pltpu.make_async_copy(saved_h, raw, in_sem.at[0]),
            pltpu.make_async_copy(fx_h, fx.at[pl.ds(0, layers)], in_sem.at[1]),
            pltpu.make_async_copy(cot_h, adj, in_sem.at[2]),
            pltpu.make_async_copy(fy_h, fy.at[:, data], in_sem.at[3]),
            pltpu.make_async_copy(fz_h, fz, in_sem.at[4]),
            pltpu.make_async_copy(rhs_h, rhs, in_sem.at[5]),
        ]
        for load in loads:
            load.start()

        barrier = pltpu.get_barrier_semaphore()
        pl.semaphore_signal(barrier, inc=1, device_id={"gx": near},
                            device_id_type=pl.DeviceIdType.MESH)

        @pl.when(has_far)
        def _():
            pl.semaphore_signal(barrier, inc=1, device_id={"gx": far},
                                device_id_type=pl.DeviceIdType.MESH)

        def halo(buf, which, k, side, c):
            layer, there, device = (
                (near_layer, high - near_halo, near) if side == 0
                else (far_layer, high - far_halo, far)
            )
            part = pl.ds(pl.multiple_of(PAD + c * ROWS, PAD), ROWS)
            return pltpu.make_async_remote_copy(
                src_ref=buf.at[k, layer, part],
                dst_ref=buf.at[k, there, part],
                send_sem=send_sem.at[which, k, side, c],
                recv_sem=recv_sem.at[which, k, side, c],
                device_id={"gx": device},
                device_id_type=pl.DeviceIdType.MESH,
            )

        def on_side(side, action):
            if side == 0:
                action()
            else:
                pl.when(has_far)(action)

        chunks = ny // ROWS

        def send(buf, which, k, side, c):
            on_side(side, lambda: halo(buf, which, k, side, c).start())

        def receive(buf, which, k, side, c):
            on_side(side, lambda: halo(buf, which, k, side, c).wait_recv())

        def each(first, end, action):
            def step(i, carry):
                action(i)
                return carry

            lax.fori_loop(first, end, step, 0)

        face_copy = pltpu.make_async_remote_copy(
            src_ref=fx.at[0], dst_ref=fx.at[layers],
            send_sem=edge_send.at[0], recv_sem=edge_recv.at[0],
            device_id={"gx": me - 1}, device_id_type=pl.DeviceIdType.MESH)
        def diag_copy(c):
            part = pl.ds(pl.multiple_of(PAD + c * ROWS, PAD), ROWS)
            return pltpu.make_async_remote_copy(
                src_ref=db.at[top, part], dst_ref=db.at[0, part],
                send_sem=diag_send.at[c], recv_sem=diag_recv.at[c],
                device_id={"gx": me + 1}, device_id_type=pl.DeviceIdType.MESH)

        strip = jnp.zeros((PAD, nz), f32)

        def clear_pads(l, carry):
            for k in range(STEPS):
                for buf in (u, p):
                    buf[k, l + 1, pl.ds(0, PAD), :] = strip
                    buf[k, l + 1, pl.ds(PAD + ny, PAD), :] = strip
            fy[l, pl.ds(PAD + ny, PAD), :] = strip
            db[l + 1, pl.ds(0, PAD), :] = strip
            return carry

        lax.fori_loop(0, layers, clear_pads, 0)

        @pl.when(jnp.logical_not(has_far))
        def _():
            def clear(r, carry):
                for k in range(STEPS):
                    for buf in (u, p):
                        buf[k, far_halo, pl.ds(PAD + r * PAD, PAD), :] = strip
                return carry

            lax.fori_loop(0, ny // PAD, clear, 0)

        @pl.when(jnp.logical_not(has_above))
        def _():
            def clear(r, carry):
                fx[layers, pl.ds(r * PAD, PAD), :] = strip
                return carry

            lax.fori_loop(0, ny // PAD, clear, 0)

        @pl.when(jnp.logical_not(has_below))
        def _():
            def clear(r, carry):
                db[0, pl.ds(PAD + r * PAD, PAD), :] = strip
                return carry

            lax.fori_loop(0, ny // PAD, clear, 0)

        lane = lax.broadcasted_iota(jnp.int32, (ROWS, nz), 1)
        first_lane, last_lane = lane == 0, lane == nz - 1

        def lower_z(x):
            return jnp.where(first_lane, 0.0, pltpu.roll(x, 1, 1))

        def upper_z(x):
            return jnp.where(last_lane, 0.0, pltpu.roll(x, nz - 1, 1))

        def lower_y(load, r):
            tall = load(pl.ds(pl.multiple_of(r, PAD), ROWS + PAD))
            return pltpu.roll(tall, 1, 0)[PAD:]

        def upper_y(load, r):
            tall = load(pl.ds(pl.multiple_of(PAD + r, PAD), ROWS + PAD))
            return pltpu.roll(tall, ROWS + PAD - 1, 0)[:ROWS]

        def over_rows(body, l):
            each(0, chunks, lambda c: body(l, pl.multiple_of(c * ROWS, ROWS), c))

        def stencil(buf, k, l, r):
            here = buf[k, l, pl.ds(PAD + r, ROWS), :]
            flow = fx[l - 1, pl.ds(r, ROWS), :] * (here - buf[k, l - 1, pl.ds(PAD + r, ROWS), :])
            flow += fx[l, pl.ds(r, ROWS), :] * (here - buf[k, l + 1, pl.ds(PAD + r, ROWS), :])
            flow += fy[l - 1, pl.ds(PAD + r, ROWS), :] * (
                here - lower_y(lambda i: buf[k, l, i, :], r))
            flow += upper_y(lambda i: fy[l - 1, i, :], r) * (
                here - upper_y(lambda i: buf[k, l, i, :], r))
            along = fz[l - 1, pl.ds(r, ROWS), :] * (here - lower_z(here))
            return here, flow + (along - upper_z(along))

        def widen(l, r):
            u[0, l, pl.ds(PAD + r, ROWS), :] = raw[l - 1, pl.ds(r, ROWS), :].astype(f32)

        def prepare(l, r):
            rows = pl.ds(r, ROWS)
            across = fz[l - 1, rows, :]
            diagonal = (
                fx[l - 1, rows, :] + fx[l, rows, :]
                + fy[l - 1, pl.ds(PAD + r, ROWS), :]
                + upper_y(lambda i: fy[l - 1, i, :], r)
                + across + upper_z(across)
            )
            inverse = 1.0 / diagonal
            rd[l - 1, rows, :] = inverse
            seed = adj[l - 1, rows, :]
            cb[l - 1, rows, :] = seed
            p[last, l, pl.ds(PAD + r, ROWS), :] = (-coefs[last][1]) * seed * inverse

        def forward(k, l, r):
            rows = pl.ds(r, ROWS)
            here, flow = stencil(u, k, l, r)
            scaled = (rhs[l - 1, rows, :] - flow) * rd[l - 1, rows, :]
            z[k, l - 1, rows, :] = scaled
            if k < last:
                change = coefs[k][1] * scaled
                if k > 0:
                    change += coefs[k][0] * d[l - 1, rows, :]
                d[l - 1, rows, :] = change
                u[k + 1, l, pl.ds(PAD + r, ROWS), :] = here + change

        def backward(k, l, r):
            rows = pl.ds(r, ROWS)
            here, flow = stencil(p, k, l, r)
            total = adj[l - 1, rows, :] + flow
            adj[l - 1, rows, :] = total
            if k > 0:
                change = total + coefs[k][0] * cb[l - 1, rows, :]
                cb[l - 1, rows, :] = change
                p[k - 1, l, pl.ds(PAD + r, ROWS), :] = (
                    (-coefs[k - 1][1]) * change * rd[l - 1, rows, :])

        def grads(l, r, steps):
            sums = [None, None, None]
            for k in steps:
                mine = pl.ds(PAD + r, ROWS)
                a, b = u[k, l, mine, :], p[k, l, mine, :]
                terms = (
                    (a - u[k, l - 1, mine, :]) * (b - p[k, l - 1, mine, :]),
                    (a - lower_y(lambda i: u[k, l, i, :], r))
                    * (b - lower_y(lambda i: p[k, l, i, :], r)),
                    (a - lower_z(a)) * (b - lower_z(b)),
                )
                sums = [t if s is None else s + t for s, t in zip(sums, terms)]
            return sums

        def middle_grads(l, r):
            rows = pl.ds(r, ROWS)
            for out, value in zip((gx, gy, gz), grads(l, r, (1, 2))):
                out[l - 1, rows, :] = value

        def diag_bar(l, r):
            mine = pl.ds(PAD + r, ROWS)
            total = p[0, l, mine, :] * z[0, l - 1, pl.ds(r, ROWS), :]
            for k in range(1, STEPS):
                total += p[k, l, mine, :] * z[k, l - 1, pl.ds(r, ROWS), :]
            db[l, mine, :] = total

        def end_grads(l, r):
            rows, mine = pl.ds(r, ROWS), pl.ds(PAD + r, ROWS)
            x, y, across = grads(l, r, (0, last))
            extra = db[l, mine, :]
            gx[l - 1, rows, :] += x + (extra + db[l - 1, mine, :])
            gy[l - 1, rows, :] += y + (extra + lower_y(lambda i: db[l, i, :], r))
            gz[l - 1, rows, :] += across + (extra + lower_z(extra))

        def rows_of(action, l):
            each(0, chunks, lambda c: action(l, pl.multiple_of(c * ROWS, ROWS)))

        def layers_of(first, end, action):
            each(first, end, lambda l: rows_of(action, l))

        def first_send(buf, which, k):
            for side in (1, 0):
                each(0, chunks, lambda c: send(buf, which, k, side, c))

        loads[0].wait()
        layers_of(1, top + 1, widen)
        @pl.when(has_far)
        def _():
            pl.semaphore_wait(barrier, 2)

        @pl.when(jnp.logical_not(has_far))
        def _():
            pl.semaphore_wait(barrier, 1)

        loads[1].wait()
        pl.when(has_below)(face_copy.start)
        first_send(u, 0, 0)
        for load in loads[2:5]:
            load.wait()
        layers_of(1, top, prepare)
        pl.when(has_above)(face_copy.wait_recv)
        rows_of(prepare, top)
        first_send(p, 1, last)
        loads[5].wait()

        def halo_step(k, side, layer, buf, which, step, following):
            def chunk(c):
                receive(buf, which, k, side, c)
                step(k, layer, pl.multiple_of(c * ROWS, ROWS))
                if following is not None:
                    send(buf, which, following, side, c)

            each(0, chunks, chunk)

        for k in range(last):
            back = last - k
            layers_of(2, top, lambda l, r: forward(k, l, r))
            layers_of(2, top, lambda l, r: backward(back, l, r))
            for side, layer in ((0, near_layer), (1, far_layer)):
                halo_step(k, side, layer, u, 0, forward, k + 1)
                halo_step(back, side, layer, p, 1, backward, back - 1)

        def finish(l):
            rows_of(end_grads, l)

        def close(k, l, r):
            forward(k, l, r)
            diag_bar(l, r)

        layers_of(2, top, lambda l, r: close(last, l, r))
        layers_of(2, top, lambda l, r: backward(0, l, r))
        layers_of(1, top + 1, middle_grads)
        halo_step(last, 0, near_layer, u, 0, close, None)

        @pl.when(jnp.logical_and(core == 0, has_above))
        def _():
            each(0, chunks, lambda c: diag_copy(c).start())

        halo_step(0, 0, near_layer, p, 1, backward, None)
        each(3 - core, top + 1 - core, finish)

        def far_chunk(c):
            receive(u, 0, last, 1, c)
            close(last, far_layer, pl.multiple_of(c * ROWS, ROWS))

            @pl.when(jnp.logical_and(core == 1, has_above))
            def _():
                diag_copy(c).start()

        each(0, chunks, far_chunk)
        finish(2 + (top - 2) * core)
        halo_step(0, 1, far_layer, p, 1, backward, None)

        def last_chunk(c):
            @pl.when(has_below)
            def _():
                diag_copy(c).wait_recv()

            end_grads(1, pl.multiple_of(c * ROWS, ROWS))

        each(0, chunks, last_chunk)

        for which, buf in ((0, u), (1, p)):
            for k in range(STEPS):
                for side in range(2):
                    each(0, chunks, lambda c: on_side(
                        side, lambda: halo(buf, which, k, side, c).wait_send()))
        pl.when(has_below)(face_copy.wait_send)

        @pl.when(has_above)
        def _():
            each(0, chunks, lambda c: diag_copy(c).wait_send())

    return kernel


def per_device(saved_field, right_side, face_x, face_y, face_z, cotangent):
    layers, ny, nz = face_x.shape
    n = lax.axis_size("gx")
    block = (layers, ny, nz)
    tall = ny + 2 * PAD

    def vmem(shape, dtype=jnp.float32):
        return pltpu.VMEM(shape, dtype)

    out = jax.ShapeDtypeStruct(block, jnp.float32)
    return pl.pallas_call(
        make_kernel(n, layers, ny, nz),
        out_shape=(out,) * 4,
        in_specs=[pl.BlockSpec(memory_space=pl.ANY)] * 6,
        out_specs=[pl.BlockSpec(memory_space=pltpu.VMEM)] * 4,
        scratch_shapes=[
            vmem((STEPS, layers + 2, tall, nz)),
            vmem((STEPS, layers + 2, tall, nz)),
            vmem((layers + 1, ny, nz)),
            vmem((layers, tall, nz)),
            vmem(block),
            vmem(block),
            vmem(block),
            vmem(block),
            vmem(block),
            vmem((STEPS,) + block),
            vmem((layers + 1, tall, nz)),
            vmem(block, jnp.bfloat16),
            pltpu.SemaphoreType.DMA((6,)),
            pltpu.SemaphoreType.DMA((2, STEPS, 2, ny // ROWS)),
            pltpu.SemaphoreType.DMA((2, STEPS, 2, ny // ROWS)),
            pltpu.SemaphoreType.DMA((1,)),
            pltpu.SemaphoreType.DMA((1,)),
            pltpu.SemaphoreType.DMA((ny // ROWS,)),
            pltpu.SemaphoreType.DMA((ny // ROWS,)),
        ],
        compiler_params=pltpu.CompilerParams(
            collective_id=0, has_side_effects=True, vmem_limit_bytes=50 * 1024 * 1024
        ),
        cost_estimate=pl.CostEstimate(
            flops=300 * layers * ny * nz, bytes_accessed=38 * layers * ny * nz, transcendentals=0
        ),
    )(saved_field, right_side, face_x, face_y, face_z, cotangent)


def solution(mesh):
    spec = P(("grp", "gx"), None, None)
    return jax.shard_map(
        per_device, mesh=mesh, in_specs=(spec,) * 6, out_specs=(spec,) * 4, check_vma=False
    )
```

```python
import jax
import jax.numpy as jnp
from jax import lax
from jax.experimental import pallas as pl
from jax.experimental.pallas import tpu as pltpu
from jax.sharding import PartitionSpec as P

STEPS = 4
ROWS = 64
PAD = 8

spectrum_low = 0.25
spectrum_high = 2.05


def chebyshev(count):
    centre = (spectrum_high + spectrum_low) / 2.0
    half = (spectrum_high - spectrum_low) / 2.0
    ratio = centre / half
    rho_prev = 1.0 / ratio
    coefs = [(0.0, 1.0 / centre)]
    for index in range(1, count):
        rho_next = 1.0 / (2.0 * ratio - rho_prev)
        coefs.append((rho_next * rho_prev, 2.0 * rho_next / half))
        rho_prev = rho_next
    return coefs


def make_kernel(n, layers, ny, nz):
    coefs = chebyshev(STEPS)
    top = layers
    high = layers + 1
    last = STEPS - 1
    f32 = jnp.float32

    def kernel(saved_h, rhs_h, fx_h, fy_h, fz_h, cot_h, adj, gx, gy, gz,
               u, p, fx, fy, fz, rd, rhs, d, cb, z, db, raw,
               in_sem, send_sem, recv_sem, edge_send, edge_recv,
               diag_send, diag_recv):
        me = lax.axis_index("gx")
        core = me % 2
        near, far = me + 1 - 2 * core, me - 1 + 2 * core
        near_layer, far_layer = top - (top - 1) * core, 1 + (top - 1) * core
        near_halo, far_halo = high * (1 - core), high * core
        has_far = jnp.logical_and(far >= 0, far < n)
        has_below, has_above = me > 0, me < n - 1
        data = pl.ds(PAD, ny)

        loads = [
            pltpu.make_async_copy(saved_h, raw, in_sem.at[0]),
            pltpu.make_async_copy(fx_h, fx.at[pl.ds(0, layers)], in_sem.at[1]),
            pltpu.make_async_copy(cot_h, adj, in_sem.at[2]),
            pltpu.make_async_copy(fy_h, fy.at[:, data], in_sem.at[3]),
            pltpu.make_async_copy(fz_h, fz, in_sem.at[4]),
            pltpu.make_async_copy(rhs_h, rhs, in_sem.at[5]),
        ]
        for load in loads:
            load.start()

        barrier = pltpu.get_barrier_semaphore()
        pl.semaphore_signal(barrier, inc=1, device_id={"gx": near},
                            device_id_type=pl.DeviceIdType.MESH)

        @pl.when(has_far)
        def _():
            pl.semaphore_signal(barrier, inc=1, device_id={"gx": far},
                                device_id_type=pl.DeviceIdType.MESH)

        def halo(buf, which, k, side, c):
            layer, there, device = (
                (near_layer, high - near_halo, near) if side == 0
                else (far_layer, high - far_halo, far)
            )
            part = pl.ds(pl.multiple_of(PAD + c * ROWS, PAD), ROWS)
            return pltpu.make_async_remote_copy(
                src_ref=buf.at[k, layer, part],
                dst_ref=buf.at[k, there, part],
                send_sem=send_sem.at[which, k, side, c],
                recv_sem=recv_sem.at[which, k, side, c],
                device_id={"gx": device},
                device_id_type=pl.DeviceIdType.MESH,
            )

        def on_side(side, action):
            if side == 0:
                action()
            else:
                pl.when(has_far)(action)

        chunks = ny // ROWS

        def send(buf, which, k, side, c):
            on_side(side, lambda: halo(buf, which, k, side, c).start())

        def receive(buf, which, k, side, c):
            on_side(side, lambda: halo(buf, which, k, side, c).wait_recv())

        def each(first, end, action):
            def step(i, carry):
                action(i)
                return carry

            lax.fori_loop(first, end, step, 0)

        face_copy = pltpu.make_async_remote_copy(
            src_ref=fx.at[0], dst_ref=fx.at[layers],
            send_sem=edge_send.at[0], recv_sem=edge_recv.at[0],
            device_id={"gx": me - 1}, device_id_type=pl.DeviceIdType.MESH)
        def diag_copy(c):
            part = pl.ds(pl.multiple_of(PAD + c * ROWS, PAD), ROWS)
            return pltpu.make_async_remote_copy(
                src_ref=db.at[top, part], dst_ref=db.at[0, part],
                send_sem=diag_send.at[c], recv_sem=diag_recv.at[c],
                device_id={"gx": me + 1}, device_id_type=pl.DeviceIdType.MESH)

        strip = jnp.zeros((PAD, nz), f32)

        def clear_pads(l, carry):
            for k in range(STEPS):
                for buf in (u, p):
                    buf[k, l + 1, pl.ds(0, PAD), :] = strip
                    buf[k, l + 1, pl.ds(PAD + ny, PAD), :] = strip
            fy[l, pl.ds(PAD + ny, PAD), :] = strip
            db[l + 1, pl.ds(0, PAD), :] = strip
            return carry

        lax.fori_loop(0, layers, clear_pads, 0)

        @pl.when(jnp.logical_not(has_far))
        def _():
            def clear(r, carry):
                for k in range(STEPS):
                    for buf in (u, p):
                        buf[k, far_halo, pl.ds(PAD + r * PAD, PAD), :] = strip
                return carry

            lax.fori_loop(0, ny // PAD, clear, 0)

        @pl.when(jnp.logical_not(has_above))
        def _():
            def clear(r, carry):
                fx[layers, pl.ds(r * PAD, PAD), :] = strip
                return carry

            lax.fori_loop(0, ny // PAD, clear, 0)

        @pl.when(jnp.logical_not(has_below))
        def _():
            def clear(r, carry):
                db[0, pl.ds(PAD + r * PAD, PAD), :] = strip
                return carry

            lax.fori_loop(0, ny // PAD, clear, 0)

        lane = lax.broadcasted_iota(jnp.int32, (ROWS, nz), 1)
        first_lane, last_lane = lane == 0, lane == nz - 1

        def lower_z(x):
            return jnp.where(first_lane, 0.0, pltpu.roll(x, 1, 1))

        def upper_z(x):
            return jnp.where(last_lane, 0.0, pltpu.roll(x, nz - 1, 1))

        def lower_y(load, r):
            tall = load(pl.ds(pl.multiple_of(r, PAD), ROWS + PAD))
            return pltpu.roll(tall, 1, 0)[PAD:]

        def upper_y(load, r):
            tall = load(pl.ds(pl.multiple_of(PAD + r, PAD), ROWS + PAD))
            return pltpu.roll(tall, ROWS + PAD - 1, 0)[:ROWS]

        def over_rows(body, l):
            each(0, chunks, lambda c: body(l, pl.multiple_of(c * ROWS, ROWS), c))

        def stencil(buf, k, l, r):
            here = buf[k, l, pl.ds(PAD + r, ROWS), :]
            flow = fx[l - 1, pl.ds(r, ROWS), :] * (here - buf[k, l - 1, pl.ds(PAD + r, ROWS), :])
            flow += fx[l, pl.ds(r, ROWS), :] * (here - buf[k, l + 1, pl.ds(PAD + r, ROWS), :])
            flow += fy[l - 1, pl.ds(PAD + r, ROWS), :] * (
                here - lower_y(lambda i: buf[k, l, i, :], r))
            flow += upper_y(lambda i: fy[l - 1, i, :], r) * (
                here - upper_y(lambda i: buf[k, l, i, :], r))
            along = fz[l - 1, pl.ds(r, ROWS), :] * (here - lower_z(here))
            return here, flow + (along - upper_z(along))

        def widen(l, r):
            u[0, l, pl.ds(PAD + r, ROWS), :] = raw[l - 1, pl.ds(r, ROWS), :].astype(f32)

        def prepare(l, r):
            rows = pl.ds(r, ROWS)
            across = fz[l - 1, rows, :]
            diagonal = (
                fx[l - 1, rows, :] + fx[l, rows, :]
                + fy[l - 1, pl.ds(PAD + r, ROWS), :]
                + upper_y(lambda i: fy[l - 1, i, :], r)
                + across + upper_z(across)
            )
            inverse = 1.0 / diagonal
            rd[l - 1, rows, :] = inverse
            seed = adj[l - 1, rows, :]
            cb[l - 1, rows, :] = seed
            p[last, l, pl.ds(PAD + r, ROWS), :] = (-coefs[last][1]) * seed * inverse

        def forward(k, l, r):
            rows = pl.ds(r, ROWS)
            here, flow = stencil(u, k, l, r)
            scaled = (rhs[l - 1, rows, :] - flow) * rd[l - 1, rows, :]
            z[k, l - 1, rows, :] = scaled
            if k < last:
                change = coefs[k][1] * scaled
                if k > 0:
                    change += coefs[k][0] * d[l - 1, rows, :]
                d[l - 1, rows, :] = change
                u[k + 1, l, pl.ds(PAD + r, ROWS), :] = here + change

        def backward(k, l, r):
            rows = pl.ds(r, ROWS)
            here, flow = stencil(p, k, l, r)
            total = adj[l - 1, rows, :] + flow
            adj[l - 1, rows, :] = total
            if k > 0:
                change = total + coefs[k][0] * cb[l - 1, rows, :]
                cb[l - 1, rows, :] = change
                p[k - 1, l, pl.ds(PAD + r, ROWS), :] = (
                    (-coefs[k - 1][1]) * change * rd[l - 1, rows, :])

        def grads(l, r, steps):
            sums = [None, None, None]
            for k in steps:
                mine = pl.ds(PAD + r, ROWS)
                a, b = u[k, l, mine, :], p[k, l, mine, :]
                terms = (
                    (a - u[k, l - 1, mine, :]) * (b - p[k, l - 1, mine, :]),
                    (a - lower_y(lambda i: u[k, l, i, :], r))
                    * (b - lower_y(lambda i: p[k, l, i, :], r)),
                    (a - lower_z(a)) * (b - lower_z(b)),
                )
                sums = [t if s is None else s + t for s, t in zip(sums, terms)]
            return sums

        def middle_grads(l, r):
            rows = pl.ds(r, ROWS)
            for out, value in zip((gx, gy, gz), grads(l, r, (1, 2))):
                out[l - 1, rows, :] = value

        def diag_bar(l, r):
            mine = pl.ds(PAD + r, ROWS)
            total = p[0, l, mine, :] * z[0, l - 1, pl.ds(r, ROWS), :]
            for k in range(1, STEPS):
                total += p[k, l, mine, :] * z[k, l - 1, pl.ds(r, ROWS), :]
            db[l, mine, :] = total

        def end_grads(l, r):
            rows, mine = pl.ds(r, ROWS), pl.ds(PAD + r, ROWS)
            x, y, across = grads(l, r, (0, last))
            extra = db[l, mine, :]
            gx[l - 1, rows, :] += x + (extra + db[l - 1, mine, :])
            gy[l - 1, rows, :] += y + (extra + lower_y(lambda i: db[l, i, :], r))
            gz[l - 1, rows, :] += across + (extra + lower_z(extra))

        def rows_of(action, l):
            each(0, chunks, lambda c: action(l, pl.multiple_of(c * ROWS, ROWS)))

        def layers_of(first, end, action):
            each(first, end, lambda l: rows_of(action, l))

        def first_send(buf, which, k):
            for side in (1, 0):
                each(0, chunks, lambda c: send(buf, which, k, side, c))

        loads[0].wait()
        layers_of(1, top + 1, widen)
        @pl.when(has_far)
        def _():
            pl.semaphore_wait(barrier, 2)

        @pl.when(jnp.logical_not(has_far))
        def _():
            pl.semaphore_wait(barrier, 1)

        loads[1].wait()
        pl.when(has_below)(face_copy.start)
        first_send(u, 0, 0)
        for load in loads[2:5]:
            load.wait()
        layers_of(1, top, prepare)
        pl.when(has_above)(face_copy.wait_recv)
        rows_of(prepare, top)
        first_send(p, 1, last)
        loads[5].wait()

        def halo_step(k, side, layer, buf, which, step, following):
            def chunk(c):
                receive(buf, which, k, side, c)
                step(k, layer, pl.multiple_of(c * ROWS, ROWS))
                if following is not None:
                    send(buf, which, following, side, c)

            each(0, chunks, chunk)

        for k in range(last):
            back = last - k
            layers_of(2, top, lambda l, r: forward(k, l, r))
            halo_step(k, 0, near_layer, u, 0, forward, k + 1)
            halo_step(k, 1, far_layer, u, 0, forward, k + 1)
            layers_of(2, top, lambda l, r: backward(back, l, r))
            halo_step(back, 0, near_layer, p, 1, backward, back - 1)
            halo_step(back, 1, far_layer, p, 1, backward, back - 1)

        def finish(l):
            rows_of(end_grads, l)

        def close(k, l, r):
            forward(k, l, r)
            diag_bar(l, r)

        layers_of(2, top, lambda l, r: close(last, l, r))
        layers_of(2, top, lambda l, r: backward(0, l, r))
        layers_of(1, top + 1, middle_grads)
        halo_step(last, 0, near_layer, u, 0, close, None)

        @pl.when(jnp.logical_and(core == 0, has_above))
        def _():
            each(0, chunks, lambda c: diag_copy(c).start())

        halo_step(0, 0, near_layer, p, 1, backward, None)
        each(3 - core, top + 1 - core, finish)

        def far_chunk(c):
            receive(u, 0, last, 1, c)
            close(last, far_layer, pl.multiple_of(c * ROWS, ROWS))

            @pl.when(jnp.logical_and(core == 1, has_above))
            def _():
                diag_copy(c).start()

        each(0, chunks, far_chunk)
        finish(2 + (top - 2) * core)
        halo_step(0, 1, far_layer, p, 1, backward, None)

        def last_chunk(c):
            @pl.when(has_below)
            def _():
                diag_copy(c).wait_recv()

            end_grads(1, pl.multiple_of(c * ROWS, ROWS))

        each(0, chunks, last_chunk)

        for which, buf in ((0, u), (1, p)):
            for k in range(STEPS):
                for side in range(2):
                    each(0, chunks, lambda c: on_side(
                        side, lambda: halo(buf, which, k, side, c).wait_send()))
        pl.when(has_below)(face_copy.wait_send)

        @pl.when(has_above)
        def _():
            each(0, chunks, lambda c: diag_copy(c).wait_send())

    return kernel


def per_device(saved_field, right_side, face_x, face_y, face_z, cotangent):
    layers, ny, nz = face_x.shape
    n = lax.axis_size("gx")
    block = (layers, ny, nz)
    tall = ny + 2 * PAD

    def vmem(shape, dtype=jnp.float32):
        return pltpu.VMEM(shape, dtype)

    out = jax.ShapeDtypeStruct(block, jnp.float32)
    return pl.pallas_call(
        make_kernel(n, layers, ny, nz),
        out_shape=(out,) * 4,
        in_specs=[pl.BlockSpec(memory_space=pl.ANY)] * 6,
        out_specs=[pl.BlockSpec(memory_space=pltpu.VMEM)] * 4,
        scratch_shapes=[
            vmem((STEPS, layers + 2, tall, nz)),
            vmem((STEPS, layers + 2, tall, nz)),
            vmem((layers + 1, ny, nz)),
            vmem((layers, tall, nz)),
            vmem(block),
            vmem(block),
            vmem(block),
            vmem(block),
            vmem(block),
            vmem((STEPS,) + block),
            vmem((layers + 1, tall, nz)),
            vmem(block, jnp.bfloat16),
            pltpu.SemaphoreType.DMA((6,)),
            pltpu.SemaphoreType.DMA((2, STEPS, 2, ny // ROWS)),
            pltpu.SemaphoreType.DMA((2, STEPS, 2, ny // ROWS)),
            pltpu.SemaphoreType.DMA((1,)),
            pltpu.SemaphoreType.DMA((1,)),
            pltpu.SemaphoreType.DMA((ny // ROWS,)),
            pltpu.SemaphoreType.DMA((ny // ROWS,)),
        ],
        compiler_params=pltpu.CompilerParams(
            collective_id=0, has_side_effects=True, vmem_limit_bytes=50 * 1024 * 1024
        ),
        cost_estimate=pl.CostEstimate(
            flops=300 * layers * ny * nz, bytes_accessed=38 * layers * ny * nz, transcendentals=0
        ),
    )(saved_field, right_side, face_x, face_y, face_z, cotangent)


def solution(mesh):
    spec = P(("grp", "gx"), None, None)
    return jax.shard_map(
        per_device, mesh=mesh, in_specs=(spec,) * 6, out_specs=(spec,) * 4, check_vma=False
    )
```
